128 devices in a mesh: cluster: 4 (over z), member: 32 (over y, x, core).
Axes of the slice: x: 4, y: 4, z: 4, core: 2. Of those that a mesh axis runs over, the one named last changes fastest.
Arguments:
- embeddings: bfloat16 [32768, 768], P(('cluster', 'member')), may hold values from -6 to 6
- destination: int32 [32768, 1], P(('cluster', 'member')), may hold values from 0 to 127; in each aligned block of 256 rows (0 to 255, 256 to 511, ...) at most 4 rows name the same one
Outputs:
- dup_score: float32 [32768], P(('cluster', 'member'))
The draws below stay inside these ranges and needn't reach their ends.
Inputs may be any that keep to these rules, and one draw needn't show every extreme that they name: In the rows of one device, no destination is named more than 4 times, a bound that some block reaches.
All inputs are finite; a program needn't handle non-finite values.
Results may differ from the reference program's by a relative error of at most 0.0003.
Values may be sent and summed in bfloat16 or wider, within the bound.
No kernel may reach another device: no remote copies, remote signals or barrier semaphores. Data moves between devices by JAX's collectives and lax.ppermute only.
A program may use at most 128 MiB of HBM per device.

```python
import math
import jax
import jax.numpy as jnp
import numpy as np
from jax import lax

D = 768
ROWS_DEV = 256
MEMBERS = 32
SEND_CAP = 4
ROWS = 32768
DEVICES = 128


def shard_levels(own_key, extent, split, smallest, largest):
    def one(axis_at, blocks):
        heights = jax.random.uniform(jax.random.fold_in(jax.random.fold_in(own_key, 6), axis_at), (blocks,), jnp.float32, smallest / len(split), largest / len(split))
        return jnp.repeat(jnp.exp(heights), extent[axis_at] // blocks).reshape((-1,) + (1,) * (len(extent) - axis_at - 1))

    level = one(*split[0])
    for cut in split[1:]:
        level = level * one(*cut)
    return level


def assign_block(key, own, number, rows, count, top, limit, skew):
    order = jax.random.permutation(key, count)
    crowded, ordinary = load_shares(count, rows * top, limit, skew, True), load_shares(count, rows * top, limit, skew, False)
    places = jnp.arange(count)

    def named(tallies, offset_by):
        used = int((tallies > 0).sum())
        fixed = max(1, used // 4)
        shifted = fixed + (places - fixed + offset_by * (used - fixed)) % max(1, count - fixed)
        return jnp.zeros((count,), jnp.int32).at[order[jnp.where(places < fixed, places, shifted)]].set(jnp.asarray(tallies, jnp.int32))

    tallies = jnp.where(number % 4 == 0, named(crowded, number // 4), named(ordinary, number - number // 4 - 1))
    mixed = jax.random.permutation(jax.random.fold_in(own, 3), count)
    donor, receiver = mixed[0:count // 2 * 2:2], mixed[1:count // 2 * 2:2]
    room = jnp.minimum(tallies[donor] - 1, limit - tallies[receiver]) // 2
    room = jnp.where((donor == order[0]) | (receiver == order[0]) | (tallies[receiver] == 0), 0, jnp.maximum(room, 0))
    shifted = jax.random.randint(jax.random.fold_in(own, 4), (count // 2,), 0, 1 << 20) % (room + 1)
    tallies = tallies.at[donor].add(-shifted).at[receiver].add(shifted)
    items = jnp.searchsorted(jnp.cumsum(tallies), jnp.arange(rows * top), side="right").astype(jnp.int32)
    table = items.reshape(top, rows).T
    table = table[jax.random.permutation(jax.random.fold_in(own, 1), rows)]
    offset_by = jax.random.randint(jax.random.fold_in(own, 2), (rows, 1), 0, top)
    return jnp.take_along_axis(table, (jnp.arange(top)[None, :] + offset_by) % top, axis=1)


def load_shares(count, total, limit, slope, full):
    weights = [(1 << 20) // math.isqrt(grade ** slope) + 1 for grade in range(1, count + 1)]
    largest = limit if full else min(limit, max(-(-total // count), total * weights[0] // sum(weights)))
    least = 1 if total - largest >= count - 1 else 0
    given, surplus = [largest] + [least] * (count - 1), total - largest - least * (count - 1)
    while surplus > 0:
        movable = [i for i in range(1, count) if given[i] < largest] or [i for i in range(1, count) if given[i] < limit]
        whole, remaining = sum([weights[i] for i in movable]), surplus
        for i in movable:
            extra = min(limit - given[i], max(1, remaining * weights[i] // whole), surplus)
            given[i] = given[i] + extra
            surplus = surplus - extra
    return np.array(given)


def noise(own_key, dims, scale, limit, split=(), kind=jnp.bfloat16):
    result = scale * jax.random.normal(own_key, dims, jnp.float32)
    if split:
        result = result * shard_levels(own_key, dims, split, -0.22, 0.18)
    return jnp.clip(result, -limit, limit).astype(kind)


def setup_inputs(seed: int = 0) -> dict:
    splits = jax.random.split(jax.random.key(seed), 3)
    embeddings = noise(splits[0], (ROWS, D), 1.0, 6.0, ((0, 128),))
    destination_keys = jax.random.split(jax.random.fold_in(splits[1], 1), ROWS // ROWS_DEV)
    destination_turns = jax.random.permutation(jax.random.fold_in(splits[1], 3), ROWS // ROWS_DEV)
    destination = jax.vmap(lambda own, number: assign_block(jax.random.fold_in(splits[1], 2), own, number, ROWS_DEV, DEVICES, 1, SEND_CAP, 2))(destination_keys, destination_turns).reshape((ROWS, 1))
    return dict(embeddings=embeddings, destination=destination)


sharpness = 30.0

def reference(embeddings, destination):
    row_count = embeddings.shape[0]
    vectors = embeddings.astype(jnp.float32)
    unit_rows = (vectors * lax.rsqrt(lax.optimization_barrier(jnp.sum(vectors * vectors, axis=1, keepdims=True)) + 1e-06)).astype(jnp.bfloat16)
    cluster_ids = destination[:, 0] // MEMBERS
    block_rows = math.gcd(row_count, 1024)
    all_ids = jnp.arange(row_count, dtype=jnp.int32)

    def block_density(first_row):
        local_units = lax.dynamic_slice_in_dim(unit_rows, first_row, block_rows, 0)
        local_ids = lax.dynamic_slice_in_dim(cluster_ids, first_row, block_rows, 0)
        scores = jnp.dot(local_units, unit_rows.T, preferred_element_type=jnp.float32)
        row_ids = first_row + jnp.arange(block_rows, dtype=jnp.int32)
        matching = (local_ids[:, None] == cluster_ids[None, :]) & (row_ids[:, None] != all_ids[None, :])
        return lax.optimization_barrier(jnp.sum(jnp.where(matching, jnp.exp(sharpness * scores), jnp.zeros_like(scores)), axis=1))
    starts = jnp.arange(row_count // block_rows, dtype=jnp.int32) * block_rows
    density = lax.map(block_density, starts).reshape(row_count)
    return jnp.log1p(density)
```

```python
import functools
import math

import jax
import jax.numpy as jnp
import numpy as np
from jax import lax
from jax.experimental import pallas as pl
from jax.experimental.pallas import tpu as pltpu
from jax.sharding import PartitionSpec as P

sharpness = 30.0
EXP2_SCALE = sharpness * math.log2(math.e)
ROWS, WIDTH, LABEL_ROWS, LANES = 256, 768, 16, 128
BOTH = ("cluster", "member")
CLUSTER_SHIFT = 5

PLAN = (
    (0, 5, 51),
    (0, 28, 28),
    (0, 51, 5),
    (3, 48, 4),
    (3, 12, 3),
    (1, 12, 48),
    (0, 3, 1),
    (2, 16, 16),
    (1, 4, 12),
    (0, 4, 3),
)


def shift(place, by):
    return sum(((place >> s) + (by >> s) & 3) << s for s in (0, 2, 4))


def minus(place):
    return sum((-(place >> s) & 3) << s for s in (0, 2, 4))


def device(place, core):
    x, y, z = place & 3, place >> 2 & 3, place >> 4
    return ((z * 4 + y) * 4 + x) * 2 + core


def fetch(jumps):
    return [(device(shift(p, jumps[c]), c), device(p, c)) for p in range(64) for c in (0, 1)]


def give(jumps):
    return [(b, a) for a, b in fetch(jumps)]


CORE_SWAP = [(d, d ^ 1) for d in range(128)]


def held_offsets():
    held = ([0], [0])
    for source, *jumps in PLAN:
        for core in (0, 1):
            held[core].append(shift(held[core][source], jumps[core]))
    return held


HELD = held_offsets()
BLOCKS = len(HELD[0])
OFFSETS = sorted(HELD[0])
assert OFFSETS == sorted(HELD[1])


def slot(core, offset, kind):
    return HELD[kind].index(offset) + (0 if core == kind else BLOCKS)


def class_pairs():
    found = {}
    for a in OFFSETS:
        for b in OFFSETS:
            d = shift(a, minus(b))
            if d and minus(d) not in found and d not in found:
                found[d] = (a, b)
    assert len(found) == 35
    return found


def tables():
    wide, narrow = [], []
    for variant in range(16):
        core, high = variant & 1, variant >> 1
        w, n = [], []
        for d, (a, b) in class_pairs().items():
            if d == minus(d):
                bit = next(i for i in range(3) if d >> (2 * i) & 3 == 2)
                kind = high >> bit & 1
                ka, kb = (0, 1) if core == 0 else (kind, kind)
                n.append((slot(core, a, ka), slot(core, b, kb)))
            else:
                w.append((slot(core, a, core), slot(core, b, 0), slot(core, b, 1)))
        wide.append(w)
        narrow.append(n)
    return np.array(wide, np.int32), np.array(narrow, np.int32)


def pack_body(rows_ref, target_ref, out_ref):
    vectors = rows_ref[...].astype(jnp.float32)
    norms = jnp.sum(vectors * vectors, axis=1, keepdims=True)
    out_ref[0:ROWS, :] = (vectors * lax.rsqrt(norms + 1e-06)).astype(jnp.bfloat16)
    labels = (target_ref[...] >> CLUSTER_SHIFT).astype(jnp.float32)
    columns = jnp.broadcast_to(labels, (ROWS, LANES))
    out_ref[ROWS:, :] = jnp.zeros((LABEL_ROWS, WIDTH), jnp.bfloat16)
    for half in range(ROWS // LANES):
        part = slice(half * LANES, (half + 1) * LANES)
        out_ref[ROWS:, part] = columns[part].T[0:LABEL_ROWS].astype(jnp.bfloat16)


def pack(embeddings, destination):
    return pl.pallas_call(
        pack_body,
        out_shape=jax.ShapeDtypeStruct((ROWS + LABEL_ROWS, WIDTH), jnp.bfloat16),
        name="pack",
    )(embeddings, destination)


def halves():
    return [slice(h * LANES, (h + 1) * LANES) for h in range(ROWS // LANES)]


def pairs_body(slots, wide_count, narrow_count, variant_ref, wide_ref, narrow_ref, *refs):
    blocks, out_ref = refs[:slots], refs[slots]
    held, row_labels, column_labels, row_sums, column_sums, arrived = refs[slots + 1 :]
    variant = variant_ref[0]
    copies = [pltpu.make_async_copy(blocks[k], held.at[k], arrived.at[k]) for k in range(slots)]
    for copy in copies:
        copy.start()
    row_sums[...] = jnp.zeros_like(row_sums)
    column_sums[...] = jnp.zeros_like(column_sums)
    for k in range(slots):
        copies[k].wait()
        labels = held[k, ROWS:, 0:ROWS].astype(jnp.float32)
        row_labels[k] = labels[0:8]
        for part in halves():
            column_labels[k, part, :] = jnp.broadcast_to(labels[0:1, part], (LANES, LANES)).T

    def weights(a, b):
        scores = lax.dot_general(
            held[a, 0:ROWS], held[b, 0:ROWS], (((1,), (1,)), ((), ())), preferred_element_type=jnp.float32
        )
        left = column_labels[a]
        return [
            jnp.where(left == row_labels[b, 0:1, part], jnp.exp2(scores[:, part] * EXP2_SCALE), 0.0)
            for part in halves()
        ]

    def add_columns(b, values):
        for part, value in zip(halves(), values):
            column_sums[b, :, part] += jnp.sum(value.reshape(ROWS // 8, 8, LANES), axis=0)

    def wide_unit(i, _):
        at = (variant * wide_count + i) * 3
        a = wide_ref[at]
        total = row_sums[a]
        for b in (wide_ref[at + 1], wide_ref[at + 2]):
            values = weights(a, b)
            total += values[0] + values[1]
            add_columns(b, values)
        row_sums[a] = total
        return 0

    def narrow_unit(i, _):
        at = (variant * narrow_count + i) * 2
        a, b = narrow_ref[at], narrow_ref[at + 1]
        values = weights(a, b)
        row_sums[a] += values[0] + values[1]
        add_columns(b, values)
        return 0

    lax.fori_loop(0, wide_count, wide_unit, 0)
    lax.fori_loop(0, narrow_count, narrow_unit, 0)

    own = weights(0, 0)
    rows = lax.broadcasted_iota(jnp.int32, (ROWS, LANES), 0)
    lanes = lax.broadcasted_iota(jnp.int32, (ROWS, LANES), 1)
    for h in range(len(own)):
        row_sums[0] += jnp.where(rows == lanes + h * LANES, 0.0, own[h])

    @pl.when(lax.rem(variant, 2) == 0)
    def _():
        values = weights(0, BLOCKS)
        row_sums[0] += values[0] + values[1]
        add_columns(BLOCKS, values)

    for k in range(slots):
        for part in halves():
            by_lane = jnp.sum(row_sums[k, part, :].T, axis=0, keepdims=True)
            out_ref[k : k + 1, part] = by_lane + jnp.sum(column_sums[k, :, part], axis=0, keepdims=True)


def pair_sums(variant, blocks):
    wide, narrow = tables()
    slots = len(blocks)
    smem, anywhere = pl.BlockSpec(memory_space=pltpu.SMEM), pl.BlockSpec(memory_space=pl.ANY)
    units = 2 * wide.shape[1] + narrow.shape[1] + 2
    return pl.pallas_call(
        functools.partial(pairs_body, slots, wide.shape[1], narrow.shape[1]),
        out_shape=jax.ShapeDtypeStruct((slots, ROWS), jnp.float32),
        in_specs=[smem] * 3 + [anywhere] * slots,
        out_specs=pl.BlockSpec(memory_space=pltpu.VMEM),
        scratch_shapes=[
            pltpu.VMEM((slots, ROWS + LABEL_ROWS, WIDTH), jnp.bfloat16),
            pltpu.VMEM((slots, 8, ROWS), jnp.float32),
            pltpu.VMEM((slots, ROWS, LANES), jnp.float32),
            pltpu.VMEM((slots, ROWS, LANES), jnp.float32),
            pltpu.VMEM((slots, 8, ROWS), jnp.float32),
            pltpu.SemaphoreType.DMA((slots,)),
        ],
        compiler_params=pltpu.CompilerParams(vmem_limit_bytes=32 * 1024 * 1024),
        cost_estimate=pl.CostEstimate(
            flops=2 * units * ROWS * ROWS * WIDTH,
            bytes_accessed=2 * slots * ROWS * WIDTH,
            transcendentals=units * ROWS * ROWS,
        ),
        name="pair_sums",
    )(variant, jnp.asarray(wide.reshape(-1)), jnp.asarray(narrow.reshape(-1)), *blocks)


def shards(embeddings, destination):
    member = lax.axis_index("member")
    core = member & 1
    place = (member >> 1) + 16 * lax.axis_index("cluster")
    high = (place >> 1 & 1) + 2 * (place >> 3 & 1) + 4 * (place >> 5 & 1)
    variant = (core + 2 * high).astype(jnp.int32).reshape(1)

    mine = [pack(embeddings, destination)]
    for source, *jumps in PLAN:
        mine.append(lax.ppermute(mine[source], BOTH, fetch(jumps)))
    others = [lax.ppermute(block, BOTH, CORE_SWAP) for block in mine]
    sums = pair_sums(variant, mine + others)

    shares = [OFFSETS[1::2], OFFSETS[2::2]]
    assert len(shares[0]) == len(shares[1])

    def rows_of(offsets_of, kind_of):
        by_core = [
            np.array([slot(c, offset, kind) for offset in offsets_of(c) for kind in kind_of(c)], np.int32)
            for c in (0, 1)
        ]
        index = jnp.where(core == 0, jnp.asarray(by_core[0]), jnp.asarray(by_core[1]))
        return jnp.take(sums, index, axis=0)

    kinds = lambda c: (0, 1)
    kept = rows_of(lambda c: shares[c], kinds)
    given = rows_of(lambda c: shares[1 - c], kinds)
    kept = (kept + lax.ppermute(given, BOTH, CORE_SWAP)).reshape(-1, 2 * ROWS)
    home = jnp.where(core == 0, sums[0], sums[BLOCKS]), jnp.where(core == 0, sums[BLOCKS], sums[0])
    total = jnp.concatenate(home)
    for k in range(len(shares[0])):
        total += lax.ppermute(kept[k : k + 1], BOTH, give((shares[0][k], shares[1][k])))[0]
    total = total.reshape(2, ROWS)
    own = jnp.where(core == 0, total[0], total[1])
    other = jnp.where(core == 0, total[1], total[0])
    density = own + lax.ppermute(other, BOTH, CORE_SWAP)
    return jnp.log1p(density)


def solution(mesh):
    in_specs = (P(BOTH, None), P(BOTH, None))
    return jax.shard_map(shards, mesh=mesh, in_specs=in_specs, out_specs=P(BOTH), check_vma=False)
```

```python
import functools
import math

import jax
import jax.numpy as jnp
import numpy as np
from jax import lax
from jax.experimental import pallas as pl
from jax.experimental.pallas import tpu as pltpu
from jax.sharding import PartitionSpec as P

sharpness = 30.0
EXP2_SCALE = sharpness * math.log2(math.e)
ROWS, WIDTH, LABEL_ROWS, LANES = 256, 768, 16, 128
BOTH = ("cluster", "member")
CLUSTER_SHIFT = 5

PLAN = ((0, 5), (0, 60), (0, 17), (0, 3), (2, 3), (3, 12), (4, 16), (1, 48), (4, 4), (3, 4))
SWAPPED = 7
BLOCKS = len(PLAN) + 1
PHASES = ((5, 5), (BLOCKS, SWAPPED))


def shift(place, by):
    return sum(((place >> s) + (by >> s) & 3) << s for s in (0, 2, 4))


def minus(place):
    return sum((-(place >> s) & 3) << s for s in (0, 2, 4))


def mirror(place, core=1):
    return place & 3 | (place >> 4) << 2 | (place >> 2 & 3) << 4 if core else place


def device(place, core):
    x, y, z = place & 3, place >> 2 & 3, place >> 4
    return ((z * 4 + y) * 4 + x) * 2 + core


def fetch(jumps):
    return [(device(shift(p, jumps[c]), c), device(p, c)) for p in range(64) for c in (0, 1)]


def give(jumps):
    return [(b, a) for a, b in fetch(jumps)]


CORE_SWAP = [(d, d ^ 1) for d in range(128)]


def held_offsets():
    held = [0]
    for source, jump in PLAN:
        held.append(shift(held[source], jump))
    return held


HELD = held_offsets()
assert len(set(HELD)) == BLOCKS and {mirror(o) for o in HELD} == set(HELD)


def units():
    lists, seen = [], set()
    for mine, other in PHASES:
        found = [("self", 0, True, 0, None)] if not lists else []
        for b in range(mine):
            for a in range(b):
                d = shift(HELD[a], minus(HELD[b]))
                if (0, d) not in seen:
                    seen.update({(0, d), (0, minus(d))})
                    axis = next((i for i in range(3) if d >> (2 * i) & 3 == 2), None)
                    found.append(("full" if d != minus(d) else "half", a, True, b, axis))
        for b in range(other):
            for a in range(mine):
                d = shift(HELD[a], minus(mirror(HELD[b])))
                if (1, d) not in seen:
                    seen.update({(1, d), (1, minus(mirror(d)))})
                    found.append(("full" if d != minus(mirror(d)) else "half", a, False, b, None))
        lists.append(sorted(found, key=lambda unit: unit[1]))
    assert len(seen) == 63 + 64
    return lists


UNITS = units()


def pack_body(rows_ref, target_ref, out_ref):
    vectors = rows_ref[...].astype(jnp.float32)
    norms = jnp.sum(vectors * vectors, axis=1, keepdims=True)
    out_ref[0:ROWS, :] = (vectors * lax.rsqrt(norms + 1e-06)).astype(jnp.bfloat16)
    labels = (target_ref[...] >> CLUSTER_SHIFT).astype(jnp.float32)
    out_ref[ROWS:, 0:ROWS] = jnp.broadcast_to(labels, (LABEL_ROWS, ROWS)).astype(jnp.bfloat16)
    out_ref[ROWS:, ROWS:] = jnp.zeros((LABEL_ROWS, WIDTH - ROWS), jnp.bfloat16)


def pack(embeddings, destination):
    return pl.pallas_call(
        pack_body,
        out_shape=jax.ShapeDtypeStruct((ROWS + LABEL_ROWS, WIDTH), jnp.bfloat16),
        name="pack",
    )(embeddings, destination.reshape(1, ROWS))


def parts(start=0):
    return [slice(start + s, start + s + LANES) for s in range(0, ROWS - start, LANES)]


def pairs_body(work, mine_used, other_used, earlier, place_ref, *refs):
    count = len(mine_used) + len(other_used)
    mine = dict(zip(mine_used, refs))
    other = dict(zip(other_used, refs[len(mine_used) : count]))
    before_ref = refs[count] if earlier else None
    out_ref, labels_ref, row_sums, column_sums = refs[count + earlier :]
    firsts = sorted({a for _, a, *_ in work})
    at = {a: n for n, a in enumerate(firsts)}
    row_sums[...] = jnp.zeros_like(row_sums)
    column_sums[...] = jnp.zeros_like(column_sums)

    def row_labels(ref):
        return ref[ROWS:, 0:ROWS].astype(jnp.float32)[0:1]

    for a in firsts:
        labels = row_labels(mine[a])
        for part in parts():
            labels_ref[at[a], part, :] = jnp.broadcast_to(labels[:, part], (LANES, LANES)).T

    def weights(a, a_rows, b_ref, b_rows, b_labels):
        scores = lax.dot_general(
            mine[a][a_rows], b_ref[b_rows], (((1,), (1,)), ((), ())), preferred_element_type=jnp.float32
        )
        left = labels_ref[at[a], a_rows, :]
        return [
            jnp.where(left == right, jnp.exp2(scores[:, n * LANES : (n + 1) * LANES] * EXP2_SCALE), 0.0)
            for n, right in enumerate(b_labels)
        ]

    def down(value):
        return jnp.sum(value.reshape(-1, 8, LANES), axis=0)

    for kind, a, is_mine, b, axis in work:
        b_ref = mine[b] if is_mine else other[b]
        slot = b if is_mine else BLOCKS + b
        labels = row_labels(b_ref)
        everything = slice(0, ROWS)
        if kind == "half":
            low, high = parts()
            (value,) = weights(a, low, b_ref, high, [labels[:, high]])
            row_sums[at[a], low, :] += value
            column_sums[slot, :, high] += down(value)
            which = place_ref[0] if axis is None else place_ref[1 + axis]
            same = pl.ds(pl.multiple_of(which * LANES, LANES), LANES)
            chosen = jnp.where(which == 0, labels[:, low], labels[:, high])
            (value,) = weights(a, same, b_ref, same, [chosen])
            row_sums[at[a], same, :] += value
            column_sums[slot, :, same] += down(value)
            continue
        values = weights(a, everything, b_ref, everything, [labels[:, part] for part in parts()])
        if kind == "self":
            rows = lax.broadcasted_iota(jnp.int32, (ROWS, LANES), 0)
            lanes = lax.broadcasted_iota(jnp.int32, (ROWS, LANES), 1)
            values = [jnp.where(rows == lanes + n * LANES, 0.0, value) for n, value in enumerate(values)]
        else:
            for part, value in zip(parts(), values):
                column_sums[slot, :, part] += down(value)
        row_sums[at[a]] += values[0] + values[1]

    for slot in range(2 * BLOCKS):
        for part in parts():
            total = jnp.sum(column_sums[slot, :, part], axis=0, keepdims=True)
            if slot in at:
                total += jnp.sum(row_sums[at[slot], part, :].T, axis=0, keepdims=True)
            if earlier:
                total += before_ref[slot : slot + 1, part]
            out_ref[slot : slot + 1, part] = total


def pair_sums(phase, place, mine, other, before):
    work = UNITS[phase]
    mine_used = sorted({a for _, a, *_ in work} | {b for _, _, is_mine, b, _ in work if is_mine})
    other_used = sorted({b for _, _, is_mine, b, _ in work if not is_mine})
    blocks = [mine[k] for k in mine_used] + [other[k] for k in other_used]
    blocks = [pltpu.with_memory_space_constraint(block, pltpu.VMEM) for block in blocks]
    before = [] if before is None else [before]
    smem, vmem = pl.BlockSpec(memory_space=pltpu.SMEM), pl.BlockSpec(memory_space=pltpu.VMEM)
    firsts = len({a for _, a, *_ in work})
    area = sum(ROWS * ROWS // (2 if kind == "half" else 1) for kind, *_ in work)
    return pl.pallas_call(
        functools.partial(pairs_body, work, mine_used, other_used, len(before)),
        out_shape=jax.ShapeDtypeStruct((2 * BLOCKS, ROWS), jnp.float32),
        in_specs=[smem] + [vmem] * (len(blocks) + len(before)),
        out_specs=vmem,
        scratch_shapes=[
            pltpu.VMEM((firsts, ROWS, LANES), jnp.float32),
            pltpu.VMEM((firsts, ROWS, LANES), jnp.float32),
            pltpu.VMEM((2 * BLOCKS, 8, ROWS), jnp.float32),
        ],
        compiler_params=pltpu.CompilerParams(vmem_limit_bytes=24 * 1024 * 1024),
        cost_estimate=pl.CostEstimate(flops=2 * area * WIDTH, bytes_accessed=0, transcendentals=area),
        name=f"pair_sums_{phase}",
    )(place, *blocks, *before)


def shards(embeddings, destination):
    member = lax.axis_index("member")
    core = member & 1
    chip = (member >> 1) + 16 * lax.axis_index("cluster")
    x, y, z = (chip >> s & 1 for s in (1, 3, 5))
    place = jnp.stack([core, x, jnp.where(core == 0, y, z), jnp.where(core == 0, z, y)]).astype(jnp.int32)

    mine = [pack(embeddings, destination)]
    for source, jump in PLAN:
        mine.append(lax.ppermute(mine[source], BOTH, fetch((jump, mirror(jump)))))
    other = [lax.ppermute(block, BOTH, CORE_SWAP) for block in mine[:SWAPPED]]
    sums = None
    for phase in range(len(PHASES)):
        sums = pair_sums(phase, place, mine, other, sums)

    offsets = sorted(HELD)[1:]
    shares = [offsets[0::2], offsets[1::2]]

    def rows_of(share_of):
        by_core = []
        for c in (0, 1):
            places = [(mirror(o, c), mirror(o, 1 - c)) for o in share_of(c)]
            slots = [(HELD.index(a), BLOCKS + HELD.index(b)) for a, b in places]
            by_core.append(np.array([pair[::-1] if c else pair for pair in slots], np.int32).reshape(-1))
        index = jnp.where(core == 0, jnp.asarray(by_core[0]), jnp.asarray(by_core[1]))
        return jnp.take(sums, index, axis=0)

    kept = rows_of(lambda c: shares[c])
    given = rows_of(lambda c: shares[1 - c])
    kept = (kept + lax.ppermute(given, BOTH, CORE_SWAP)).reshape(-1, 2 * ROWS)
    total = jnp.where(core == 0, jnp.stack([sums[0], sums[BLOCKS]]), jnp.stack([sums[BLOCKS], sums[0]])).reshape(-1)
    for k in range(len(shares[0])):
        total += lax.ppermute(kept[k : k + 1], BOTH, give((shares[0][k], shares[1][k])))[0]
    total = total.reshape(2, ROWS)
    own = jnp.where(core == 0, total[0], total[1])
    rest = jnp.where(core == 0, total[1], total[0])
    density = own + lax.ppermute(rest, BOTH, CORE_SWAP)
    return jnp.log1p(density)


def solution(mesh):
    in_specs = (P(BOTH, None), P(BOTH, None))
    return jax.shard_map(shards, mesh=mesh, in_specs=in_specs, out_specs=P(BOTH), check_vma=False)
```

```python
import functools
import math

import jax
import jax.numpy as jnp
import numpy as np
from jax import lax
from jax.experimental import pallas as pl
from jax.experimental.pallas import tpu as pltpu
from jax.sharding import PartitionSpec as P

sharpness = 30.0
EXP2_SCALE = sharpness * math.log2(math.e)
ROWS, WIDTH, LABEL_ROWS, LANES = 256, 768, 16, 128
BOTH = ("cluster", "member")
CLUSTER_SHIFT = 5

PLAN = ((0, 13), (0, 20), (0, 3), (0, 49), (1, 48), (1, 16), (2, 3), (3, 48), (4, 4), (3, 12))
SWAPPED = 7
BLOCKS = len(PLAN) + 1
PHASES = ((5, 5), (7, 7), (BLOCKS, SWAPPED))


def shift(place, by):
    return sum(((place >> s) + (by >> s) & 3) << s for s in (0, 2, 4))


def minus(place):
    return sum((-(place >> s) & 3) << s for s in (0, 2, 4))


def mirror(place, core=1):
    return place & 3 | (place >> 4) << 2 | (place >> 2 & 3) << 4 if core else place


def device(place, core):
    x, y, z = place & 3, place >> 2 & 3, place >> 4
    return ((z * 4 + y) * 4 + x) * 2 + core


def fetch(jumps):
    return [(device(shift(p, jumps[c]), c), device(p, c)) for p in range(64) for c in (0, 1)]


def give(jumps):
    return [(b, a) for a, b in fetch(jumps)]


CORE_SWAP = [(d, d ^ 1) for d in range(128)]


def held_offsets():
    held = [0]
    for source, jump in PLAN:
        held.append(shift(held[source], jump))
    return held


HELD = held_offsets()
assert len(set(HELD)) == BLOCKS and {mirror(o) for o in HELD} == set(HELD)


def distance(place):
    return sum(min(place >> s & 3, -(place >> s) & 3) for s in (0, 2, 4))


AFAR = sorted(sorted(HELD)[1:], key=distance, reverse=True)
SHARES = (AFAR[0::2], AFAR[1::2])
SHARE = len(SHARES[0])
GIVEN, HOME = 16, 32


def table_row(core, slot):
    kind = core if slot < BLOCKS else 1 - core
    offset = mirror(HELD[slot % BLOCKS], kind)
    if offset == 0:
        return HOME + kind
    own = offset in SHARES[core]
    return 2 * SHARES[core if own else 1 - core].index(offset) + kind + (0 if own else GIVEN)


def units():
    lists, seen = [], set()
    for mine, other in PHASES:
        found = [("self", 0, True, 0, None)] if not lists else []
        for b in range(mine):
            for a in range(b):
                d = shift(HELD[a], minus(HELD[b]))
                if (0, d) not in seen:
                    seen.update({(0, d), (0, minus(d))})
                    axis = next((i for i in range(3) if d >> (2 * i) & 3 == 2), None)
                    found.append(("full" if d != minus(d) else "half", a, True, b, axis))
        for b in range(other):
            for a in range(mine):
                d = shift(HELD[a], minus(mirror(HELD[b])))
                if (1, d) not in seen:
                    seen.update({(1, d), (1, minus(mirror(d)))})
                    found.append(("full" if d != minus(mirror(d)) else "half", a, False, b, None))
        lists.append(sorted(found, key=lambda unit: unit[1]))
    assert len(seen) == 63 + 64
    return lists


UNITS = units()


def pack_body(rows_ref, target_ref, out_ref):
    vectors = rows_ref[...].astype(jnp.float32)
    norms = jnp.sum(vectors * vectors, axis=1, keepdims=True)
    out_ref[0:ROWS, :] = (vectors * lax.rsqrt(norms + 1e-06)).astype(jnp.bfloat16)
    labels = (target_ref[...] >> CLUSTER_SHIFT).astype(jnp.float32)
    out_ref[ROWS:, 0:ROWS] = jnp.broadcast_to(labels, (LABEL_ROWS, ROWS)).astype(jnp.bfloat16)
    out_ref[ROWS:, ROWS:] = jnp.zeros((LABEL_ROWS, WIDTH - ROWS), jnp.bfloat16)


def pack(embeddings, destination):
    return pl.pallas_call(
        pack_body,
        out_shape=jax.ShapeDtypeStruct((ROWS + LABEL_ROWS, WIDTH), jnp.bfloat16),
        name="pack",
    )(embeddings, destination.reshape(1, ROWS))


def parts(start=0):
    return [slice(start + s, start + s + LANES) for s in range(0, ROWS - start, LANES)]


def pairs_body(work, mine_used, other_used, earlier, last, place_ref, *refs):
    count = len(mine_used) + len(other_used)
    mine = dict(zip(mine_used, refs))
    other = dict(zip(other_used, refs[len(mine_used) : count]))
    before_ref = refs[count] if earlier else None
    outs, (labels_ref, row_sums, column_sums, table) = refs[count + earlier : -4], refs[-4:]
    firsts = sorted({a for _, a, *_ in work})
    at = {a: n for n, a in enumerate(firsts)}
    row_sums[...] = jnp.zeros_like(row_sums)
    column_sums[...] = jnp.zeros_like(column_sums)

    def row_labels(ref):
        return ref[ROWS:, 0:ROWS].astype(jnp.float32)[0:1]

    for a in firsts:
        labels = row_labels(mine[a])
        for part in parts():
            labels_ref[at[a], part, :] = jnp.broadcast_to(labels[:, part], (LANES, LANES)).T

    def weights(a, a_rows, b_ref, b_rows, b_labels):
        scores = lax.dot_general(
            mine[a][a_rows], b_ref[b_rows], (((1,), (1,)), ((), ())), preferred_element_type=jnp.float32
        )
        left = labels_ref[at[a], a_rows, :]
        return [
            jnp.where(left == right, jnp.exp2(scores[:, n * LANES : (n + 1) * LANES] * EXP2_SCALE), 0.0)
            for n, right in enumerate(b_labels)
        ]

    def down(value):
        return jnp.sum(value.reshape(-1, 8, LANES), axis=0)

    for kind, a, is_mine, b, axis in work:
        b_ref = mine[b] if is_mine else other[b]
        slot = b if is_mine else BLOCKS + b
        labels = row_labels(b_ref)
        everything = slice(0, ROWS)
        if kind == "half":
            low, high = parts()
            (value,) = weights(a, low, b_ref, high, [labels[:, high]])
            row_sums[at[a], low, :] += value
            column_sums[slot, :, high] += down(value)
            which = place_ref[0] if axis is None else place_ref[1 + axis]
            same = pl.ds(pl.multiple_of(which * LANES, LANES), LANES)
            chosen = jnp.where(which == 0, labels[:, low], labels[:, high])
            (value,) = weights(a, same, b_ref, same, [chosen])
            row_sums[at[a], same, :] += value
            column_sums[slot, :, same] += down(value)
            continue
        values = weights(a, everything, b_ref, everything, [labels[:, part] for part in parts()])
        if kind == "self":
            rows = lax.broadcasted_iota(jnp.int32, (ROWS, LANES), 0)
            lanes = lax.broadcasted_iota(jnp.int32, (ROWS, LANES), 1)
            values = [jnp.where(rows == lanes + n * LANES, 0.0, value) for n, value in enumerate(values)]
        else:
            for part, value in zip(parts(), values):
                column_sums[slot, :, part] += down(value)
        row_sums[at[a]] += values[0] + values[1]

    for slot in range(2 * BLOCKS):
        if last:
            rows = [table_row(core, slot) for core in (0, 1)]
            row = jnp.where(place_ref[0] == 0, rows[0], rows[1])
        for part in parts():
            total = jnp.sum(column_sums[slot, :, part], axis=0, keepdims=True)
            if slot in at:
                total += jnp.sum(row_sums[at[slot], part, :].T, axis=0, keepdims=True)
            if earlier:
                total += before_ref[slot, :, part]
            if last:
                table[row, :, part] = total
            else:
                outs[0][slot, :, part] = total
    if last:
        outs[0][...] = table[0 : 2 * SHARE]
        outs[1][...] = table[GIVEN : GIVEN + 2 * SHARE]
        outs[2][...] = table[HOME : HOME + 2]


def pair_sums(phase, place, mine, other, before):
    work = UNITS[phase]
    mine_used = sorted({a for _, a, *_ in work} | {b for _, _, is_mine, b, _ in work if is_mine})
    other_used = sorted({b for _, _, is_mine, b, _ in work if not is_mine})
    blocks = [mine[k] for k in mine_used] + [other[k] for k in other_used]
    blocks = [pltpu.with_memory_space_constraint(block, pltpu.VMEM) for block in blocks]
    before = [] if before is None else [before]
    last = phase == len(PHASES) - 1
    outs = (2 * SHARE, 2 * SHARE, 2) if last else (2 * BLOCKS,)
    smem, vmem = pl.BlockSpec(memory_space=pltpu.SMEM), pl.BlockSpec(memory_space=pltpu.VMEM)
    firsts = len({a for _, a, *_ in work})
    area = sum(ROWS * ROWS // (2 if kind == "half" else 1) for kind, *_ in work)
    return pl.pallas_call(
        functools.partial(pairs_body, work, mine_used, other_used, len(before), last),
        out_shape=[jax.ShapeDtypeStruct((n, 1, ROWS), jnp.float32) for n in outs],
        in_specs=[smem] + [vmem] * (len(blocks) + len(before)),
        out_specs=[vmem] * len(outs),
        scratch_shapes=[
            pltpu.VMEM((firsts, ROWS, LANES), jnp.float32),
            pltpu.VMEM((firsts, ROWS, LANES), jnp.float32),
            pltpu.VMEM((2 * BLOCKS, 8, ROWS), jnp.float32),
            pltpu.VMEM((HOME + 2, 1, ROWS), jnp.float32),
        ],
        compiler_params=pltpu.CompilerParams(vmem_limit_bytes=24 * 1024 * 1024),
        cost_estimate=pl.CostEstimate(flops=2 * area * WIDTH, bytes_accessed=0, transcendentals=area),
        name=f"pair_sums_{phase}",
    )(place, *blocks, *before)


def shards(embeddings, destination):
    member = lax.axis_index("member")
    core = member & 1
    chip = (member >> 1) + 16 * lax.axis_index("cluster")
    x, y, z = (chip >> s & 1 for s in (1, 3, 5))
    place = jnp.stack([core, x, jnp.where(core == 0, y, z), jnp.where(core == 0, z, y)]).astype(jnp.int32)

    mine = [pack(embeddings, destination)]
    other = [lax.ppermute(mine[0], BOTH, CORE_SWAP)]
    for source, jump in PLAN[:-1]:
        mine.append(lax.ppermute(mine[source], BOTH, fetch((jump, mirror(jump)))))
    other += [lax.ppermute(block, BOTH, CORE_SWAP) for block in mine[1 : PHASES[0][1]]]
    (sums,) = pair_sums(0, place, mine, other, None)

    source, jump = PLAN[-1]
    source, later, sums = lax.optimization_barrier((mine[source], mine[PHASES[0][1] : SWAPPED], sums))
    mine.append(lax.ppermute(source, BOTH, fetch((jump, mirror(jump)))))
    other += [lax.ppermute(block, BOTH, CORE_SWAP) for block in later]
    (sums,) = pair_sums(1, place, mine, other, sums)
    kept, given, home = pair_sums(2, place, mine, other, sums)

    kept += lax.ppermute(given, BOTH, CORE_SWAP)
    for n in range(SHARE):
        jumps = [SHARES[c][n] for c in (0, 1)]
        home += lax.ppermute(kept[2 * n : 2 * n + 2], BOTH, give(jumps))
    home = home.reshape(2, ROWS)
    own, rest = jnp.where(core == 0, home[0], home[1]), jnp.where(core == 0, home[1], home[0])
    return jnp.log1p(own + lax.ppermute(rest, BOTH, CORE_SWAP))


def solution(mesh):
    in_specs = (P(BOTH, None), P(BOTH, None))
    return jax.shard_map(shards, mesh=mesh, in_specs=in_specs, out_specs=P(BOTH), check_vma=False)
```

```python
import functools
import math

import jax
import jax.numpy as jnp
import numpy as np
from jax import lax
from jax.experimental import pallas as pl
from jax.experimental.pallas import tpu as pltpu
from jax.sharding import PartitionSpec as P

sharpness = 30.0
EXP2_SCALE = sharpness * math.log2(math.e)
ROWS, WIDTH, LABEL_ROWS, LANES = 256, 768, 16, 128
BOTH = ("cluster", "member")
CLUSTER_SHIFT = 5

PLAN = ((0, 13), (0, 20), (0, 3), (0, 49), (1, 48), (1, 16), (2, 3), (3, 48), (4, 4), (3, 12))
SWAPPED = 7
BLOCKS = len(PLAN) + 1
PHASES = ((4, 4), (7, 4), (BLOCKS, 4), (BLOCKS, SWAPPED))


def shift(place, by):
    return sum(((place >> s) + (by >> s) & 3) << s for s in (0, 2, 4))


def minus(place):
    return sum((-(place >> s) & 3) << s for s in (0, 2, 4))


def mirror(place, core=1):
    return place & 3 | (place >> 4) << 2 | (place >> 2 & 3) << 4 if core else place


def device(place, core):
    x, y, z = place & 3, place >> 2 & 3, place >> 4
    return ((z * 4 + y) * 4 + x) * 2 + core


def fetch(jumps):
    return [(device(shift(p, jumps[c]), c), device(p, c)) for p in range(64) for c in (0, 1)]


def give(jumps):
    return [(b, a) for a, b in fetch(jumps)]


CORE_SWAP = [(d, d ^ 1) for d in range(128)]


def held_offsets():
    held = [0]
    for source, jump in PLAN:
        held.append(shift(held[source], jump))
    return held


HELD = held_offsets()
assert len(set(HELD)) == BLOCKS and {mirror(o) for o in HELD} == set(HELD)


def distance(place):
    return sum(min(place >> s & 3, -(place >> s) & 3) for s in (0, 2, 4))


AFAR = sorted(sorted(HELD)[1:], key=distance, reverse=True)
SHARES = (AFAR[0::2], AFAR[1::2])
SHARE = len(SHARES[0])
GIVEN, HOME = 16, 32


def table_row(core, slot):
    kind = core if slot < BLOCKS else 1 - core
    offset = mirror(HELD[slot % BLOCKS], kind)
    if offset == 0:
        return HOME + kind
    own = offset in SHARES[core]
    return 2 * SHARES[core if own else 1 - core].index(offset) + kind + (0 if own else GIVEN)


def units():
    lists, seen = [], set()
    for mine, other in PHASES:
        found = [("self", 0, True, 0, None)] if not lists else []
        for b in range(mine):
            for a in range(b):
                d = shift(HELD[a], minus(HELD[b]))
                if (0, d) not in seen:
                    seen.update({(0, d), (0, minus(d))})
                    axis = next((i for i in range(3) if d >> (2 * i) & 3 == 2), None)
                    found.append(("full" if d != minus(d) else "half", a, True, b, axis))
        for b in range(other):
            for a in range(mine):
                d = shift(HELD[a], minus(mirror(HELD[b])))
                if (1, d) not in seen:
                    seen.update({(1, d), (1, minus(mirror(d)))})
                    found.append(("full" if d != minus(mirror(d)) else "half", a, False, b, None))
        lists.append(sorted(found, key=lambda unit: unit[1]))
    assert len(seen) == 63 + 64
    return lists


UNITS = units()


def pack_body(rows_ref, target_ref, out_ref):
    vectors = rows_ref[...].astype(jnp.float32)
    norms = jnp.sum(vectors * vectors, axis=1, keepdims=True)
    out_ref[0:ROWS, :] = (vectors * lax.rsqrt(norms + 1e-06)).astype(jnp.bfloat16)
    labels = (target_ref[...] >> CLUSTER_SHIFT).astype(jnp.float32)
    out_ref[ROWS:, 0:ROWS] = jnp.broadcast_to(labels, (LABEL_ROWS, ROWS)).astype(jnp.bfloat16)
    out_ref[ROWS:, ROWS:] = jnp.zeros((LABEL_ROWS, WIDTH - ROWS), jnp.bfloat16)


def pack(embeddings, destination):
    return pl.pallas_call(
        pack_body,
        out_shape=pltpu.VMEM((ROWS + LABEL_ROWS, WIDTH), jnp.bfloat16),
        name="pack",
    )(embeddings, destination.reshape(1, ROWS))


def parts(start=0):
    return [slice(start + s, start + s + LANES) for s in range(0, ROWS - start, LANES)]


def pairs_body(work, mine_used, other_used, earlier, last, place_ref, *refs):
    count = len(mine_used) + len(other_used)
    mine = dict(zip(mine_used, refs))
    other = dict(zip(other_used, refs[len(mine_used) : count]))
    before_ref = refs[count] if earlier else None
    outs, (labels_ref, row_sums, column_sums, table) = refs[count + earlier : -4], refs[-4:]
    firsts = sorted({a for _, a, *_ in work})
    at = {a: n for n, a in enumerate(firsts)}
    row_sums[...] = jnp.zeros_like(row_sums)
    column_sums[...] = jnp.zeros_like(column_sums)

    def row_labels(ref):
        return ref[ROWS:, 0:ROWS].astype(jnp.float32)[0:1]

    for a in firsts:
        labels = row_labels(mine[a])
        for part in parts():
            labels_ref[at[a], part, :] = jnp.broadcast_to(labels[:, part], (LANES, LANES)).T

    def weights(a, a_rows, b_ref, b_rows, b_labels):
        scores = lax.dot_general(
            mine[a][a_rows], b_ref[b_rows], (((1,), (1,)), ((), ())), preferred_element_type=jnp.float32
        )
        left = labels_ref[at[a], a_rows, :]
        return [
            jnp.where(left == right, jnp.exp2(scores[:, n * LANES : (n + 1) * LANES] * EXP2_SCALE), 0.0)
            for n, right in enumerate(b_labels)
        ]

    def down(value):
        return jnp.sum(value.reshape(-1, 8, LANES), axis=0)

    for kind, a, is_mine, b, axis in work:
        b_ref = mine[b] if is_mine else other[b]
        slot = b if is_mine else BLOCKS + b
        labels = row_labels(b_ref)
        everything = slice(0, ROWS)
        if kind == "half":
            low, high = parts()
            (value,) = weights(a, low, b_ref, high, [labels[:, high]])
            row_sums[at[a], low, :] += value
            column_sums[slot, :, high] += down(value)
            which = place_ref[0] if axis is None else place_ref[1 + axis]
            same = pl.ds(pl.multiple_of(which * LANES, LANES), LANES)
            chosen = jnp.where(which == 0, labels[:, low], labels[:, high])
            (value,) = weights(a, same, b_ref, same, [chosen])
            row_sums[at[a], same, :] += value
            column_sums[slot, :, same] += down(value)
            continue
        values = weights(a, everything, b_ref, everything, [labels[:, part] for part in parts()])
        if kind == "self":
            rows = lax.broadcasted_iota(jnp.int32, (ROWS, LANES), 0)
            lanes = lax.broadcasted_iota(jnp.int32, (ROWS, LANES), 1)
            values = [jnp.where(rows == lanes + n * LANES, 0.0, value) for n, value in enumerate(values)]
        else:
            for part, value in zip(parts(), values):
                column_sums[slot, :, part] += down(value)
        row_sums[at[a]] += values[0] + values[1]

    for slot in range(2 * BLOCKS):
        if last:
            rows = [table_row(core, slot) for core in (0, 1)]
            row = jnp.where(place_ref[0] == 0, rows[0], rows[1])
        for part in parts():
            total = jnp.sum(column_sums[slot, :, part], axis=0, keepdims=True)
            if slot in at:
                total += jnp.sum(row_sums[at[slot], part, :].T, axis=0, keepdims=True)
            if earlier:
                total += before_ref[slot, :, part]
            if last:
                table[row, :, part] = total
            else:
                outs[0][slot, :, part] = total
    if last:
        outs[0][...] = table[0 : 2 * SHARE]
        outs[1][...] = table[GIVEN : GIVEN + 2 * SHARE]
        outs[2][...] = table[HOME : HOME + 2]


def pair_sums(phase, place, mine, other, before):
    work = UNITS[phase]
    mine_used = sorted({a for _, a, *_ in work} | {b for _, _, is_mine, b, _ in work if is_mine})
    other_used = sorted({b for _, _, is_mine, b, _ in work if not is_mine})
    blocks = [mine[k] for k in mine_used] + [other[k] for k in other_used]
    blocks = [pltpu.with_memory_space_constraint(block, pltpu.VMEM) for block in blocks]
    before = [] if before is None else [before]
    last = phase == len(PHASES) - 1
    outs = (2 * SHARE, 2 * SHARE, 2) if last else (2 * BLOCKS,)
    smem, vmem = pl.BlockSpec(memory_space=pltpu.SMEM), pl.BlockSpec(memory_space=pltpu.VMEM)
    firsts = len({a for _, a, *_ in work})
    area = sum(ROWS * ROWS // (2 if kind == "half" else 1) for kind, *_ in work)
    return pl.pallas_call(
        functools.partial(pairs_body, work, mine_used, other_used, len(before), last),
        out_shape=[jax.ShapeDtypeStruct((n, 1, ROWS), jnp.float32) for n in outs],
        in_specs=[smem] + [vmem] * (len(blocks) + len(before)),
        out_specs=[vmem] * len(outs),
        scratch_shapes=[
            pltpu.VMEM((firsts, ROWS, LANES), jnp.float32),
            pltpu.VMEM((firsts, ROWS, LANES), jnp.float32),
            pltpu.VMEM((2 * BLOCKS, 8, ROWS), jnp.float32),
            pltpu.VMEM((HOME + 2, 1, ROWS), jnp.float32),
        ],
        compiler_params=pltpu.CompilerParams(vmem_limit_bytes=24 * 1024 * 1024),
        cost_estimate=pl.CostEstimate(flops=2 * area * WIDTH, bytes_accessed=0, transcendentals=area),
        name=f"pair_sums_{phase}",
    )(place, *blocks, *before)


def shards(embeddings, destination):
    member = lax.axis_index("member")
    core = member & 1
    chip = (member >> 1) + 16 * lax.axis_index("cluster")
    x, y, z = (chip >> s & 1 for s in (1, 3, 5))
    place = jnp.stack([core, x, jnp.where(core == 0, y, z), jnp.where(core == 0, z, y)]).astype(jnp.int32)

    mine = [pack(embeddings, destination)]
    for source, jump in PLAN[:8]:
        mine.append(lax.ppermute(mine[source], BOTH, fetch((jump, mirror(jump)))))
    other = [lax.ppermute(block, BOTH, CORE_SWAP) for block in mine[0:4]]
    (sums,) = pair_sums(0, place, mine, other, None)
    held, sums = lax.optimization_barrier((mine[4], sums))
    for source, jump in PLAN[8:]:
        mine.append(lax.ppermute(held if source == 4 else mine[source], BOTH, fetch((jump, mirror(jump)))))
    (sums,) = pair_sums(1, place, mine, other, sums)
    later, sums = lax.optimization_barrier((mine[4:SWAPPED], sums))
    other += [lax.ppermute(block, BOTH, CORE_SWAP) for block in later]
    (sums,) = pair_sums(2, place, mine, other, sums)
    kept, given, home = pair_sums(3, place, mine, other, sums)

    kept += lax.ppermute(given, BOTH, CORE_SWAP)
    for n in range(SHARE):
        jumps = [SHARES[c][n] for c in (0, 1)]
        home += lax.ppermute(kept[2 * n : 2 * n + 2], BOTH, give(jumps))
    home = home.reshape(2, ROWS)
    own, rest = jnp.where(core == 0, home[0], home[1]), jnp.where(core == 0, home[1], home[0])
    return jnp.log1p(own + lax.ppermute(rest, BOTH, CORE_SWAP))


def solution(mesh):
    in_specs = (P(BOTH, None), P(BOTH, None))
    return jax.shard_map(shards, mesh=mesh, in_specs=in_specs, out_specs=P(BOTH), check_vma=False)
```

```python
import functools
import math

import jax
import jax.numpy as jnp
import numpy as np
from jax import lax
from jax.experimental import pallas as pl
from jax.experimental.pallas import tpu as pltpu
from jax.sharding import PartitionSpec as P

sharpness = 30.0
EXP2_SCALE = sharpness * math.log2(math.e)
ROWS, WIDTH, LABEL_ROWS, LANES = 256, 768, 16, 128
BOTH = ("cluster", "member")
CLUSTER_SHIFT = 5

PLAN = ((0, 13), (0, 20), (0, 3), (0, 49), (1, 48), (1, 16), (2, 3), (3, 48), (4, 4), (3, 12))
BLOCKS = len(PLAN) + 1
EARLY, LATE = (0, 1, 2, 3), (4, 5, 6)
PHASES = ((4, EARLY), (7, EARLY), (BLOCKS, EARLY), (BLOCKS, EARLY + LATE))


def shift(place, by):
    return sum(((place >> s) + (by >> s) & 3) << s for s in (0, 2, 4))


def minus(place):
    return sum((-(place >> s) & 3) << s for s in (0, 2, 4))


def mirror(place, core=1):
    return place & 3 | (place >> 4) << 2 | (place >> 2 & 3) << 4 if core else place


def device(place, core):
    x, y, z = place & 3, place >> 2 & 3, place >> 4
    return ((z * 4 + y) * 4 + x) * 2 + core


def fetch(jumps):
    return [(device(shift(p, jumps[c]), c), device(p, c)) for p in range(64) for c in (0, 1)]


def give(jumps):
    return [(b, a) for a, b in fetch(jumps)]


CORE_SWAP = [(d, d ^ 1) for d in range(128)]


def held_offsets():
    held = [0]
    for source, jump in PLAN:
        held.append(shift(held[source], jump))
    return held


HELD = held_offsets()
assert len(set(HELD)) == BLOCKS and {mirror(o) for o in HELD} == set(HELD)


def distance(place):
    return sum(min(place >> s & 3, -(place >> s) & 3) for s in (0, 2, 4))


AFAR = sorted(sorted(HELD)[1:], key=distance, reverse=True)
SHARES = (AFAR[0::2], AFAR[1::2])
SHARE = len(SHARES[0])
GIVEN, HOME = 16, 32


def table_row(core, slot):
    kind = core if slot < BLOCKS else 1 - core
    offset = mirror(HELD[slot % BLOCKS], kind)
    if offset == 0:
        return HOME + kind
    own = offset in SHARES[core]
    return 2 * SHARES[core if own else 1 - core].index(offset) + kind + (0 if own else GIVEN)


def units():
    lists, seen = [], set()
    for mine, other in PHASES:
        found = [("self", 0, True, 0, None)] if not lists else []
        for b in range(mine):
            for a in range(b):
                d = shift(HELD[a], minus(HELD[b]))
                if (0, d) not in seen:
                    seen.update({(0, d), (0, minus(d))})
                    axis = next((i for i in range(3) if d >> (2 * i) & 3 == 2), None)
                    found.append(("full" if d != minus(d) else "half", a, True, b, axis))
        for b in other:
            for a in range(mine):
                d = shift(HELD[a], minus(mirror(HELD[b])))
                if (1, d) not in seen:
                    seen.update({(1, d), (1, minus(mirror(d)))})
                    found.append(("full" if d != minus(mirror(d)) else "half", a, False, b, None))
        lists.append(sorted(found, key=lambda unit: unit[1]))
    assert len(seen) == 63 + 64
    return lists


UNITS = units()


def pack_body(rows_ref, target_ref, out_ref):
    vectors = rows_ref[...].astype(jnp.float32)
    norms = jnp.sum(vectors * vectors, axis=1, keepdims=True)
    out_ref[0:ROWS, :] = (vectors * lax.rsqrt(norms + 1e-06)).astype(jnp.bfloat16)
    labels = (target_ref[...] >> CLUSTER_SHIFT).astype(jnp.float32)
    out_ref[ROWS:, 0:ROWS] = jnp.broadcast_to(labels, (LABEL_ROWS, ROWS)).astype(jnp.bfloat16)
    out_ref[ROWS:, ROWS:] = jnp.zeros((LABEL_ROWS, WIDTH - ROWS), jnp.bfloat16)


def pack(embeddings, destination):
    return pl.pallas_call(
        pack_body,
        out_shape=pltpu.VMEM((ROWS + LABEL_ROWS, WIDTH), jnp.bfloat16),
        name="pack",
    )(embeddings, destination.reshape(1, ROWS))


def parts(start=0):
    return [slice(start + s, start + s + LANES) for s in range(0, ROWS - start, LANES)]


def pairs_body(work, mine_used, other_used, earlier, last, *refs):
    core, bits = core_index(), high_bits()
    count = len(mine_used) + len(other_used)
    mine = dict(zip(mine_used, refs))
    other = dict(zip(other_used, refs[len(mine_used) : count]))
    before_ref = refs[count] if earlier else None
    outs, (labels_ref, row_sums, column_sums, table) = refs[count + earlier : -4], refs[-4:]
    firsts = sorted({a for _, a, *_ in work})
    at = {a: n for n, a in enumerate(firsts)}
    row_sums[...] = jnp.zeros_like(row_sums)
    column_sums[...] = jnp.zeros_like(column_sums)

    def row_labels(ref):
        return ref[ROWS:, 0:ROWS].astype(jnp.float32)[0:1]

    for a in firsts:
        labels = row_labels(mine[a])
        for part in parts():
            labels_ref[at[a], part, :] = jnp.broadcast_to(labels[:, part], (LANES, LANES)).T

    def weights(a, a_rows, b_ref, b_rows, b_labels):
        scores = lax.dot_general(
            mine[a][a_rows], b_ref[b_rows], (((1,), (1,)), ((), ())), preferred_element_type=jnp.float32
        )
        left = labels_ref[at[a], a_rows, :]
        return [
            jnp.where(left == right, jnp.exp2(scores[:, n * LANES : (n + 1) * LANES] * EXP2_SCALE), 0.0)
            for n, right in enumerate(b_labels)
        ]

    def down(value):
        return jnp.sum(value.reshape(-1, 8, LANES), axis=0)

    for kind, a, is_mine, b, axis in work:
        b_ref = mine[b] if is_mine else other[b]
        slot = b if is_mine else BLOCKS + b
        labels = row_labels(b_ref)
        everything = slice(0, ROWS)
        if kind == "half":
            low, high = parts()
            (value,) = weights(a, low, b_ref, high, [labels[:, high]])
            row_sums[at[a], low, :] += value
            column_sums[slot, :, high] += down(value)
            which = core if axis is None else bits[axis]
            same = pl.ds(pl.multiple_of(which * LANES, LANES), LANES)
            chosen = jnp.where(which == 0, labels[:, low], labels[:, high])
            (value,) = weights(a, same, b_ref, same, [chosen])
            row_sums[at[a], same, :] += value
            column_sums[slot, :, same] += down(value)
            continue
        values = weights(a, everything, b_ref, everything, [labels[:, part] for part in parts()])
        if kind == "self":
            rows = lax.broadcasted_iota(jnp.int32, (ROWS, LANES), 0)
            lanes = lax.broadcasted_iota(jnp.int32, (ROWS, LANES), 1)
            values = [jnp.where(rows == lanes + n * LANES, 0.0, value) for n, value in enumerate(values)]
        else:
            for part, value in zip(parts(), values):
                column_sums[slot, :, part] += down(value)
        row_sums[at[a]] += values[0] + values[1]

    for slot in range(2 * BLOCKS):
        if last:
            rows = [table_row(c, slot) for c in (0, 1)]
            row = jnp.where(core == 0, rows[0], rows[1])
        for part in parts():
            total = jnp.sum(column_sums[slot, :, part], axis=0, keepdims=True)
            if slot in at:
                total += jnp.sum(row_sums[at[slot], part, :].T, axis=0, keepdims=True)
            if earlier:
                total += before_ref[slot, :, part]
            if last:
                table[row, :, part] = total
            else:
                outs[0][slot, :, part] = total
    if last:
        outs[0][...] = table[0 : 2 * SHARE]
        outs[1][...] = table[GIVEN : GIVEN + 2 * SHARE]
        outs[2][...] = table[HOME : HOME + 2]


def pair_sums(phase, mine, other, before):
    work = UNITS[phase]
    mine_used = sorted({a for _, a, *_ in work} | {b for _, _, is_mine, b, _ in work if is_mine})
    other_used = sorted({b for _, _, is_mine, b, _ in work if not is_mine})
    blocks = [mine[k] for k in mine_used] + [other[k] for k in other_used]
    blocks = [pltpu.with_memory_space_constraint(block, pltpu.VMEM) for block in blocks]
    before = [] if before is None else [pltpu.with_memory_space_constraint(before, pltpu.VMEM)]
    last = phase == len(PHASES) - 1
    outs = (2 * SHARE, 2 * SHARE, 2) if last else (2 * BLOCKS,)
    vmem = pl.BlockSpec(memory_space=pltpu.VMEM)
    firsts = len({a for _, a, *_ in work})
    area = sum(ROWS * ROWS // (2 if kind == "half" else 1) for kind, *_ in work)
    return pl.pallas_call(
        functools.partial(pairs_body, work, mine_used, other_used, len(before), last),
        out_shape=[pltpu.VMEM((n, 1, ROWS), jnp.float32) for n in outs],
        in_specs=[vmem] * (len(blocks) + len(before)),
        out_specs=[vmem] * len(outs),
        scratch_shapes=[
            pltpu.VMEM((firsts, ROWS, LANES), jnp.float32),
            pltpu.VMEM((firsts, ROWS, LANES), jnp.float32),
            pltpu.VMEM((2 * BLOCKS, 8, ROWS), jnp.float32),
            pltpu.VMEM((HOME + 2, 1, ROWS), jnp.float32),
        ],
        compiler_params=pltpu.CompilerParams(vmem_limit_bytes=24 * 1024 * 1024),
        cost_estimate=pl.CostEstimate(flops=2 * area * WIDTH, bytes_accessed=0, transcendentals=area),
        name=f"pair_sums_{phase}",
    )(*blocks, *before)


def core_index():
    return lax.axis_index("member") & 1


def high_bits():
    member, core = lax.axis_index("member"), core_index()
    x, y, z = member >> 2 & 1, member >> 4 & 1, lax.axis_index("cluster") >> 1
    return x, jnp.where(core == 0, y, z), jnp.where(core == 0, z, y)


def shards(embeddings, destination):
    core = core_index()
    mine = [pack(embeddings, destination)]
    for source, jump in PLAN[:8]:
        mine.append(lax.ppermute(mine[source], BOTH, fetch((jump, mirror(jump)))))
    other = {k: lax.ppermute(mine[k], BOTH, CORE_SWAP) for k in EARLY}
    (sums,) = pair_sums(0, mine, other, None)
    held, sums = lax.optimization_barrier((mine[4], sums))
    for source, jump in PLAN[8:]:
        mine.append(lax.ppermute(held if source == 4 else mine[source], BOTH, fetch((jump, mirror(jump)))))
    (sums,) = pair_sums(1, mine, other, sums)
    later, sums = lax.optimization_barrier(([mine[k] for k in LATE], sums))
    other.update({k: lax.ppermute(block, BOTH, CORE_SWAP) for k, block in zip(LATE, later)})
    (sums,) = pair_sums(2, mine, other, sums)
    kept, given, home = pair_sums(3, mine, other, sums)

    kept += lax.ppermute(given, BOTH, CORE_SWAP)
    for n in range(SHARE):
        jumps = [SHARES[c][n] for c in (0, 1)]
        home += lax.ppermute(kept[2 * n : 2 * n + 2], BOTH, give(jumps))
    home = home.reshape(2, ROWS)
    own, rest = jnp.where(core == 0, home[0], home[1]), jnp.where(core == 0, home[1], home[0])
    return jnp.log1p(own + lax.ppermute(rest, BOTH, CORE_SWAP))


def solution(mesh):
    in_specs = (P(BOTH, None), P(BOTH, None))
    return jax.shard_map(shards, mesh=mesh, in_specs=in_specs, out_specs=P(BOTH), check_vma=False)
```

```python
import functools
import math

import jax
import jax.numpy as jnp
import numpy as np
from jax import lax
from jax.experimental import pallas as pl
from jax.experimental.pallas import tpu as pltpu
from jax.sharding import PartitionSpec as P

sharpness = 30.0
EXP2_SCALE = sharpness * math.log2(math.e)
ROWS, WIDTH, LABEL_ROWS, LANES = 256, 768, 16, 128
BOTH = ("cluster", "member")
CLUSTER_SHIFT = 5

PLAN = ((0, 13), (0, 3), (0, 20), (0, 49), (1, 48), (1, 16), (3, 3), (2, 48), (4, 4), (2, 12))
BLOCKS = len(PLAN) + 1
EARLY, LATE = (0, 1, 2, 3), (4, 5, 6)
PHASES = ((4, EARLY), (7, EARLY), (BLOCKS, EARLY), (BLOCKS, EARLY + LATE))
HELD_BACK = 4


def shift(place, by):
    return sum(((place >> s) + (by >> s) & 3) << s for s in (0, 2, 4))


def minus(place):
    return sum((-(place >> s) & 3) << s for s in (0, 2, 4))


def mirror(place, core=1):
    return place & 3 | (place >> 4) << 2 | (place >> 2 & 3) << 4 if core else place


def device(place, core):
    x, y, z = place & 3, place >> 2 & 3, place >> 4
    return ((z * 4 + y) * 4 + x) * 2 + core


def fetch(jumps):
    return [(device(shift(p, jumps[c]), c), device(p, c)) for p in range(64) for c in (0, 1)]


def give(jumps):
    return [(b, a) for a, b in fetch(jumps)]


CORE_SWAP = [(d, d ^ 1) for d in range(128)]


def held_offsets():
    held = [0]
    for source, jump in PLAN:
        held.append(shift(held[source], jump))
    return held


HELD = held_offsets()
assert len(set(HELD)) == BLOCKS and {mirror(o) for o in HELD} == set(HELD)


def distance(place):
    return sum(min(place >> s & 3, -(place >> s) & 3) for s in (0, 2, 4))


AFAR = sorted(sorted(HELD)[1:], key=distance, reverse=True)
SHARES = (AFAR[0::2], AFAR[1::2])
SHARE = len(SHARES[0])
GIVEN, HOME = 16, 32


def table_row(core, slot):
    kind = core if slot < BLOCKS else 1 - core
    offset = mirror(HELD[slot % BLOCKS], kind)
    if offset == 0:
        return HOME + kind
    own = offset in SHARES[core]
    return 2 * SHARES[core if own else 1 - core].index(offset) + kind + (0 if own else GIVEN)


def units():
    lists, seen = [], set()
    for mine, other in PHASES:
        found = [("self", 0, True, 0, None)] if not lists else []
        for b in range(mine):
            for a in range(b):
                d = shift(HELD[a], minus(HELD[b]))
                if (0, d) not in seen:
                    seen.update({(0, d), (0, minus(d))})
                    axis = next((i for i in range(3) if d >> (2 * i) & 3 == 2), None)
                    found.append(("full" if d != minus(d) else "half", a, True, b, axis))
        for b in other:
            for a in range(mine):
                d = shift(HELD[a], minus(mirror(HELD[b])))
                if (1, d) not in seen:
                    seen.update({(1, d), (1, minus(mirror(d)))})
                    found.append(("full" if d != minus(mirror(d)) else "half", a, False, b, None))
        lists.append(sorted(found, key=lambda unit: unit[1]))
    assert len(seen) == 63 + 64
    return lists


UNITS = units()


def pack_body(rows_ref, target_ref, out_ref):
    vectors = rows_ref[...].astype(jnp.float32)
    norms = jnp.sum(vectors * vectors, axis=1, keepdims=True)
    out_ref[0:ROWS, :] = (vectors * lax.rsqrt(norms + 1e-06)).astype(jnp.bfloat16)
    labels = (target_ref[...] >> CLUSTER_SHIFT).astype(jnp.float32)
    out_ref[ROWS:, 0:ROWS] = jnp.broadcast_to(labels, (LABEL_ROWS, ROWS)).astype(jnp.bfloat16)
    out_ref[ROWS:, ROWS:] = jnp.zeros((LABEL_ROWS, WIDTH - ROWS), jnp.bfloat16)


def pack(embeddings, destination):
    return pl.pallas_call(
        pack_body,
        out_shape=pltpu.VMEM((ROWS + LABEL_ROWS, WIDTH), jnp.bfloat16),
        name="pack",
    )(embeddings, destination.reshape(1, ROWS))


def parts(start=0):
    return [slice(start + s, start + s + LANES) for s in range(0, ROWS - start, LANES)]


def pairs_body(work, mine_used, other_used, earlier, last, *refs):
    core, bits = core_index(), high_bits()
    count = len(mine_used) + len(other_used)
    mine = dict(zip(mine_used, refs))
    other = dict(zip(other_used, refs[len(mine_used) : count]))
    before_ref = refs[count] if earlier else None
    outs, (labels_ref, row_sums, column_sums, table) = refs[count + earlier : -4], refs[-4:]
    firsts = sorted({a for _, a, *_ in work})
    at = {a: n for n, a in enumerate(firsts)}
    row_sums[...] = jnp.zeros_like(row_sums)
    column_sums[...] = jnp.zeros_like(column_sums)

    def row_labels(ref):
        return ref[ROWS:, 0:ROWS].astype(jnp.float32)[0:1]

    for a in firsts:
        labels = row_labels(mine[a])
        for part in parts():
            labels_ref[at[a], part, :] = jnp.broadcast_to(labels[:, part], (LANES, LANES)).T

    def weights(a, a_rows, b_ref, b_rows, b_labels):
        scores = lax.dot_general(
            mine[a][a_rows], b_ref[b_rows], (((1,), (1,)), ((), ())), preferred_element_type=jnp.float32
        )
        left = labels_ref[at[a], a_rows, :]
        return [
            jnp.where(left == right, jnp.exp2(scores[:, n * LANES : (n + 1) * LANES] * EXP2_SCALE), 0.0)
            for n, right in enumerate(b_labels)
        ]

    def down(value):
        return jnp.sum(value.reshape(-1, 8, LANES), axis=0)

    for kind, a, is_mine, b, axis in work:
        b_ref = mine[b] if is_mine else other[b]
        slot = b if is_mine else BLOCKS + b
        labels = row_labels(b_ref)
        everything = slice(0, ROWS)
        if kind == "half":
            low, high = parts()
            (value,) = weights(a, low, b_ref, high, [labels[:, high]])
            row_sums[at[a], low, :] += value
            column_sums[slot, :, high] += down(value)
            which = core if axis is None else bits[axis]
            same = pl.ds(pl.multiple_of(which * LANES, LANES), LANES)
            chosen = jnp.where(which == 0, labels[:, low], labels[:, high])
            (value,) = weights(a, same, b_ref, same, [chosen])
            row_sums[at[a], same, :] += value
            column_sums[slot, :, same] += down(value)
            continue
        values = weights(a, everything, b_ref, everything, [labels[:, part] for part in parts()])
        if kind == "self":
            rows = lax.broadcasted_iota(jnp.int32, (ROWS, LANES), 0)
            lanes = lax.broadcasted_iota(jnp.int32, (ROWS, LANES), 1)
            values = [jnp.where(rows == lanes + n * LANES, 0.0, value) for n, value in enumerate(values)]
        else:
            for part, value in zip(parts(), values):
                column_sums[slot, :, part] += down(value)
        row_sums[at[a]] += values[0] + values[1]

    for slot in range(2 * BLOCKS):
        if last:
            rows = [table_row(c, slot) for c in (0, 1)]
            row = jnp.where(core == 0, rows[0], rows[1])
        for part in parts():
            total = jnp.sum(column_sums[slot, :, part], axis=0, keepdims=True)
            if slot in at:
                total += jnp.sum(row_sums[at[slot], part, :].T, axis=0, keepdims=True)
            if earlier:
                total += before_ref[slot, :, part]
            if last:
                table[row, :, part] = total
            else:
                outs[0][slot, :, part] = total
    if last:
        outs[0][...] = table[0 : 2 * SHARE]
        outs[1][...] = table[GIVEN : GIVEN + 2 * SHARE]
        outs[2][...] = table[HOME : HOME + 2]


def pair_sums(phase, mine, other, before):
    work = UNITS[phase]
    mine_used = sorted({a for _, a, *_ in work} | {b for _, _, is_mine, b, _ in work if is_mine})
    other_used = sorted({b for _, _, is_mine, b, _ in work if not is_mine})
    blocks = [mine[k] for k in mine_used] + [other[k] for k in other_used]
    blocks = [pltpu.with_memory_space_constraint(block, pltpu.VMEM) for block in blocks]
    before = [] if before is None else [pltpu.with_memory_space_constraint(before, pltpu.VMEM)]
    last = phase == len(PHASES) - 1
    outs = (2 * SHARE, 2 * SHARE, 2) if last else (2 * BLOCKS,)
    vmem = pl.BlockSpec(memory_space=pltpu.VMEM)
    firsts = len({a for _, a, *_ in work})
    area = sum(ROWS * ROWS // (2 if kind == "half" else 1) for kind, *_ in work)
    return pl.pallas_call(
        functools.partial(pairs_body, work, mine_used, other_used, len(before), last),
        out_shape=[pltpu.VMEM((n, 1, ROWS), jnp.float32) for n in outs],
        in_specs=[vmem] * (len(blocks) + len(before)),
        out_specs=[vmem] * len(outs),
        scratch_shapes=[
            pltpu.VMEM((firsts, ROWS, LANES), jnp.float32),
            pltpu.VMEM((firsts, ROWS, LANES), jnp.float32),
            pltpu.VMEM((2 * BLOCKS, 8, ROWS), jnp.float32),
            pltpu.VMEM((HOME + 2, 1, ROWS), jnp.float32),
        ],
        compiler_params=pltpu.CompilerParams(vmem_limit_bytes=24 * 1024 * 1024),
        cost_estimate=pl.CostEstimate(flops=2 * area * WIDTH, bytes_accessed=0, transcendentals=area),
        name=f"pair_sums_{phase}",
    )(*blocks, *before)


def core_index():
    return lax.axis_index("member") & 1


def high_bits():
    member, core = lax.axis_index("member"), core_index()
    x, y, z = member >> 2 & 1, member >> 4 & 1, lax.axis_index("cluster") >> 1
    return x, jnp.where(core == 0, y, z), jnp.where(core == 0, z, y)


def shards(embeddings, destination):
    core = core_index()
    mine = [pack(embeddings, destination)]
    mine += [None] * len(PLAN)

    def bring(k, block):
        jump = PLAN[k - 1][1]
        mine[k] = lax.ppermute(block, BOTH, fetch((jump, mirror(jump))))

    after = [k for k in range(1, BLOCKS) if PLAN[k - 1][0] == HELD_BACK]
    for k in range(1, BLOCKS):
        if k not in after:
            bring(k, mine[PLAN[k - 1][0]])
    other = {k: lax.ppermute(mine[k], BOTH, CORE_SWAP) for k in EARLY}
    (sums,) = pair_sums(0, mine, other, None)
    held, sums = lax.optimization_barrier((mine[HELD_BACK], sums))
    for k in after:
        bring(k, held)
    (sums,) = pair_sums(1, mine, other, sums)
    later, sums = lax.optimization_barrier(([mine[k] for k in LATE], sums))
    other.update({k: lax.ppermute(block, BOTH, CORE_SWAP) for k, block in zip(LATE, later)})
    (sums,) = pair_sums(2, mine, other, sums)
    kept, given, home = pair_sums(3, mine, other, sums)

    kept += lax.ppermute(given, BOTH, CORE_SWAP)
    for n in range(SHARE):
        jumps = [SHARES[c][n] for c in (0, 1)]
        home += lax.ppermute(kept[2 * n : 2 * n + 2], BOTH, give(jumps))
    density = home + lax.ppermute(home, BOTH, CORE_SWAP)
    return jnp.log1p(jnp.where(core == 0, density[0, 0], density[1, 0]))


def solution(mesh):
    in_specs = (P(BOTH, None), P(BOTH, None))
    return jax.shard_map(shards, mesh=mesh, in_specs=in_specs, out_specs=P(BOTH), check_vma=False)
```

```python
import functools
import math

import jax
import jax.numpy as jnp
import numpy as np
from jax import lax
from jax.experimental import pallas as pl
from jax.experimental.pallas import tpu as pltpu
from jax.sharding import PartitionSpec as P

sharpness = 30.0
EXP2_SCALE = sharpness * math.log2(math.e)
ROWS, WIDTH, LABEL_ROWS, LANES = 256, 768, 16, 128
BOTH = ("cluster", "member")
CLUSTER_SHIFT = 5

PLAN = ((0, 13), (0, 3), (0, 20), (0, 49), (1, 48), (1, 16), (3, 3), (2, 48), (4, 4), (2, 12))
BLOCKS = len(PLAN) + 1
EARLY, LATE = (0, 1, 2, 3), (4, 5, 6)
PHASES = ((4, EARLY), (7, EARLY), (BLOCKS, EARLY), (BLOCKS, EARLY + LATE))
HELD_BACK = 4


def shift(place, by):
    return sum(((place >> s) + (by >> s) & 3) << s for s in (0, 2, 4))


def minus(place):
    return sum((-(place >> s) & 3) << s for s in (0, 2, 4))


def mirror(place, core=1):
    return place & 3 | (place >> 4) << 2 | (place >> 2 & 3) << 4 if core else place


def device(place, core):
    x, y, z = place & 3, place >> 2 & 3, place >> 4
    return ((z * 4 + y) * 4 + x) * 2 + core


def fetch(jumps):
    return [(device(shift(p, jumps[c]), c), device(p, c)) for p in range(64) for c in (0, 1)]


def give(jumps):
    return [(b, a) for a, b in fetch(jumps)]


CORE_SWAP = [(d, d ^ 1) for d in range(128)]


def held_offsets():
    held = [0]
    for source, jump in PLAN:
        held.append(shift(held[source], jump))
    return held


HELD = held_offsets()
assert len(set(HELD)) == BLOCKS and {mirror(o) for o in HELD} == set(HELD)


SHARES = ((20, 23, 29, 13, 15), (3, 61, 53, 49, 51))
assert sorted(SHARES[0] + SHARES[1]) == sorted(HELD)[1:]
SHARE = len(SHARES[0])
GIVEN, HOME = 16, 32


def table_row(core, slot):
    kind = core if slot < BLOCKS else 1 - core
    offset = mirror(HELD[slot % BLOCKS], kind)
    if offset == 0:
        return HOME + kind
    own = offset in SHARES[core]
    return 2 * SHARES[core if own else 1 - core].index(offset) + kind + (0 if own else GIVEN)


def units():
    lists, seen = [], set()
    for mine, other in PHASES:
        found = [("self", 0, True, 0, None)] if not lists else []
        for b in range(mine):
            for a in range(b):
                d = shift(HELD[a], minus(HELD[b]))
                if (0, d) not in seen:
                    seen.update({(0, d), (0, minus(d))})
                    axis = next((i for i in range(3) if d >> (2 * i) & 3 == 2), None)
                    found.append(("full" if d != minus(d) else "half", a, True, b, axis))
        for b in other:
            for a in range(mine):
                d = shift(HELD[a], minus(mirror(HELD[b])))
                if (1, d) not in seen:
                    seen.update({(1, d), (1, minus(mirror(d)))})
                    found.append(("full" if d != minus(mirror(d)) else "half", a, False, b, None))
        lists.append(sorted(found, key=lambda unit: unit[1]))
    assert len(seen) == 63 + 64
    return lists


UNITS = units()


def pack_body(rows_ref, target_ref, out_ref):
    vectors = rows_ref[...].astype(jnp.float32)
    norms = jnp.sum(vectors * vectors, axis=1, keepdims=True)
    out_ref[0:ROWS, :] = (vectors * lax.rsqrt(norms + 1e-06)).astype(jnp.bfloat16)
    labels = (target_ref[...] >> CLUSTER_SHIFT).astype(jnp.float32)
    out_ref[ROWS:, 0:ROWS] = jnp.broadcast_to(labels, (LABEL_ROWS, ROWS)).astype(jnp.bfloat16)
    out_ref[ROWS:, ROWS:] = jnp.zeros((LABEL_ROWS, WIDTH - ROWS), jnp.bfloat16)


def pack(embeddings, destination):
    return pl.pallas_call(
        pack_body,
        out_shape=pltpu.VMEM((ROWS + LABEL_ROWS, WIDTH), jnp.bfloat16),
        name="pack",
    )(embeddings, destination.reshape(1, ROWS))


def parts(start=0):
    return [slice(start + s, start + s + LANES) for s in range(0, ROWS - start, LANES)]


def pairs_body(work, mine_used, other_used, earlier, last, *refs):
    core, bits = core_index(), high_bits()
    count = len(mine_used) + len(other_used)
    mine = dict(zip(mine_used, refs))
    other = dict(zip(other_used, refs[len(mine_used) : count]))
    before_ref = refs[count] if earlier else None
    outs, (labels_ref, row_sums, column_sums, table) = refs[count + earlier : -4], refs[-4:]
    firsts = sorted({a for _, a, *_ in work})
    at = {a: n for n, a in enumerate(firsts)}
    row_sums[...] = jnp.zeros_like(row_sums)
    column_sums[...] = jnp.zeros_like(column_sums)

    def row_labels(ref):
        return ref[ROWS:, 0:ROWS].astype(jnp.float32)[0:1]

    for a in firsts:
        labels = row_labels(mine[a])
        for part in parts():
            labels_ref[at[a], part, :] = jnp.broadcast_to(labels[:, part], (LANES, LANES)).T

    def weights(a, a_rows, b_ref, b_rows, b_labels):
        scores = lax.dot_general(
            mine[a][a_rows], b_ref[b_rows], (((1,), (1,)), ((), ())), preferred_element_type=jnp.float32
        )
        left = labels_ref[at[a], a_rows, :]
        return [
            jnp.where(left == right, jnp.exp2(scores[:, n * LANES : (n + 1) * LANES] * EXP2_SCALE), 0.0)
            for n, right in enumerate(b_labels)
        ]

    def down(value):
        return jnp.sum(value.reshape(-1, 8, LANES), axis=0)

    for kind, a, is_mine, b, axis in work:
        b_ref = mine[b] if is_mine else other[b]
        slot = b if is_mine else BLOCKS + b
        labels = row_labels(b_ref)
        everything = slice(0, ROWS)
        if kind == "half":
            low, high = parts()
            (value,) = weights(a, low, b_ref, high, [labels[:, high]])
            row_sums[at[a], low, :] += value
            column_sums[slot, :, high] += down(value)
            which = core if axis is None else bits[axis]
            same = pl.ds(pl.multiple_of(which * LANES, LANES), LANES)
            chosen = jnp.where(which == 0, labels[:, low], labels[:, high])
            (value,) = weights(a, same, b_ref, same, [chosen])
            row_sums[at[a], same, :] += value
            column_sums[slot, :, same] += down(value)
            continue
        values = weights(a, everything, b_ref, everything, [labels[:, part] for part in parts()])
        if kind == "self":
            rows = lax.broadcasted_iota(jnp.int32, (ROWS, LANES), 0)
            lanes = lax.broadcasted_iota(jnp.int32, (ROWS, LANES), 1)
            values = [jnp.where(rows == lanes + n * LANES, 0.0, value) for n, value in enumerate(values)]
        else:
            for part, value in zip(parts(), values):
                column_sums[slot, :, part] += down(value)
        row_sums[at[a]] += values[0] + values[1]

    for slot in range(2 * BLOCKS):
        if last:
            rows = [table_row(c, slot) for c in (0, 1)]
            row = jnp.where(core == 0, rows[0], rows[1])
        for part in parts():
            total = jnp.sum(column_sums[slot, :, part], axis=0, keepdims=True)
            if slot in at:
                total += jnp.sum(row_sums[at[slot], part, :].T, axis=0, keepdims=True)
            if earlier:
                total += before_ref[slot, :, part]
            if last:
                table[row, :, part] = total
            else:
                outs[0][slot, :, part] = total
    if last:
        outs[0][...] = table[0 : 2 * SHARE]
        outs[1][...] = table[GIVEN : GIVEN + 2 * SHARE]
        outs[2][...] = table[HOME : HOME + 2]


def pair_sums(phase, mine, other, before):
    work = UNITS[phase]
    mine_used = sorted({a for _, a, *_ in work} | {b for _, _, is_mine, b, _ in work if is_mine})
    other_used = sorted({b for _, _, is_mine, b, _ in work if not is_mine})
    blocks = [mine[k] for k in mine_used] + [other[k] for k in other_used]
    blocks = [pltpu.with_memory_space_constraint(block, pltpu.VMEM) for block in blocks]
    before = [] if before is None else [pltpu.with_memory_space_constraint(before, pltpu.VMEM)]
    last = phase == len(PHASES) - 1
    outs = (2 * SHARE, 2 * SHARE, 2) if last else (2 * BLOCKS,)
    vmem = pl.BlockSpec(memory_space=pltpu.VMEM)
    firsts = len({a for _, a, *_ in work})
    area = sum(ROWS * ROWS // (2 if kind == "half" else 1) for kind, *_ in work)
    return pl.pallas_call(
        functools.partial(pairs_body, work, mine_used, other_used, len(before), last),
        out_shape=[pltpu.VMEM((n, 1, ROWS), jnp.float32) for n in outs],
        in_specs=[vmem] * (len(blocks) + len(before)),
        out_specs=[vmem] * len(outs),
        scratch_shapes=[
            pltpu.VMEM((firsts, ROWS, LANES), jnp.float32),
            pltpu.VMEM((firsts, ROWS, LANES), jnp.float32),
            pltpu.VMEM((2 * BLOCKS, 8, ROWS), jnp.float32),
            pltpu.VMEM((HOME + 2, 1, ROWS), jnp.float32),
        ],
        compiler_params=pltpu.CompilerParams(vmem_limit_bytes=24 * 1024 * 1024),
        cost_estimate=pl.CostEstimate(flops=2 * area * WIDTH, bytes_accessed=0, transcendentals=area),
        name=f"pair_sums_{phase}",
    )(*blocks, *before)


def core_index():
    return lax.axis_index("member") & 1


def high_bits():
    member, core = lax.axis_index("member"), core_index()
    x, y, z = member >> 2 & 1, member >> 4 & 1, lax.axis_index("cluster") >> 1
    return x, jnp.where(core == 0, y, z), jnp.where(core == 0, z, y)


def shards(embeddings, destination):
    core = core_index()
    mine = [pack(embeddings, destination)]
    mine += [None] * len(PLAN)

    def bring(k, block):
        jump = PLAN[k - 1][1]
        mine[k] = lax.ppermute(block, BOTH, fetch((jump, mirror(jump))))

    after = [k for k in range(1, BLOCKS) if PLAN[k - 1][0] == HELD_BACK]
    for k in range(1, BLOCKS):
        if k not in after:
            bring(k, mine[PLAN[k - 1][0]])
    other = {k: lax.ppermute(mine[k], BOTH, CORE_SWAP) for k in EARLY}
    (sums,) = pair_sums(0, mine, other, None)
    held, sums = lax.optimization_barrier((mine[HELD_BACK], sums))
    for k in after:
        bring(k, held)
    (sums,) = pair_sums(1, mine, other, sums)
    later, sums = lax.optimization_barrier(([mine[k] for k in LATE], sums))
    other.update({k: lax.ppermute(block, BOTH, CORE_SWAP) for k, block in zip(LATE, later)})
    (sums,) = pair_sums(2, mine, other, sums)
    kept, given, home = pair_sums(3, mine, other, sums)

    kept += lax.ppermute(given, BOTH, CORE_SWAP)
    for n in range(SHARE):
        jumps = [SHARES[c][n] for c in (0, 1)]
        home += lax.ppermute(kept[2 * n : 2 * n + 2], BOTH, give(jumps))
    density = home + lax.ppermute(home, BOTH, CORE_SWAP)
    return jnp.log1p(jnp.where(core == 0, density[0, 0], density[1, 0]))


def solution(mesh):
    in_specs = (P(BOTH, None), P(BOTH, None))
    return jax.shard_map(shards, mesh=mesh, in_specs=in_specs, out_specs=P(BOTH), check_vma=False)
```

```python
import functools
import math

import jax
import jax.numpy as jnp
import numpy as np
from jax import lax
from jax.experimental import pallas as pl
from jax.experimental.pallas import tpu as pltpu
from jax.sharding import PartitionSpec as P

sharpness = 30.0
EXP2_SCALE = sharpness * math.log2(math.e)
ROWS, WIDTH, LABEL_ROWS, LANES = 256, 768, 16, 128
BOTH = ("cluster", "member")
CLUSTER_SHIFT = 5

PLAN = ((0, 13), (0, 3), (0, 20), (0, 49), (1, 48), (1, 16), (3, 3), (2, 48), (4, 4), (2, 12))
BLOCKS = len(PLAN) + 1
EARLY, LATE = (0, 1, 2, 3), (4, 5, 6)
PHASES = ((4, EARLY), (7, EARLY), (BLOCKS, EARLY), (BLOCKS, EARLY + LATE))
HELD_BACK = 4


def shift(place, by):
    return sum(((place >> s) + (by >> s) & 3) << s for s in (0, 2, 4))


def minus(place):
    return sum((-(place >> s) & 3) << s for s in (0, 2, 4))


def mirror(place, core=1):
    return place & 3 | (place >> 4) << 2 | (place >> 2 & 3) << 4 if core else place


def device(place, core):
    x, y, z = place & 3, place >> 2 & 3, place >> 4
    return ((z * 4 + y) * 4 + x) * 2 + core


def fetch(jumps):
    return [(device(shift(p, jumps[c]), c), device(p, c)) for p in range(64) for c in (0, 1)]


def give(jumps):
    return [(b, a) for a, b in fetch(jumps)]


CORE_SWAP = [(d, d ^ 1) for d in range(128)]


def held_offsets():
    held = [0]
    for source, jump in PLAN:
        held.append(shift(held[source], jump))
    return held


HELD = held_offsets()
assert len(set(HELD)) == BLOCKS and {mirror(o) for o in HELD} == set(HELD)


SHARES = ((20, 29, 23, 13, 15), (3, 53, 61, 49, 51))
assert sorted(SHARES[0] + SHARES[1]) == sorted(HELD)[1:]
SHARE = len(SHARES[0])
GIVEN, HOME = 16, 32


def table_row(core, slot):
    kind = core if slot < BLOCKS else 1 - core
    offset = mirror(HELD[slot % BLOCKS], kind)
    if offset == 0:
        return HOME + kind
    own = offset in SHARES[core]
    return 2 * SHARES[core if own else 1 - core].index(offset) + kind + (0 if own else GIVEN)


def units():
    lists, seen = [], set()
    for mine, other in PHASES:
        found = [("self", 0, True, 0, None)] if not lists else []
        for b in range(mine):
            for a in range(b):
                d = shift(HELD[a], minus(HELD[b]))
                if (0, d) not in seen:
                    seen.update({(0, d), (0, minus(d))})
                    axis = next((i for i in range(3) if d >> (2 * i) & 3 == 2), None)
                    found.append(("full" if d != minus(d) else "half", a, True, b, axis))
        for b in other:
            for a in range(mine):
                d = shift(HELD[a], minus(mirror(HELD[b])))
                if (1, d) not in seen:
                    seen.update({(1, d), (1, minus(mirror(d)))})
                    found.append(("full" if d != minus(mirror(d)) else "half", a, False, b, None))
        lists.append(sorted(found, key=lambda unit: unit[1]))
    assert len(seen) == 63 + 64
    return lists


UNITS = units()


def pack_body(rows_ref, target_ref, out_ref):
    vectors = rows_ref[...].astype(jnp.float32)
    norms = jnp.sum(vectors * vectors, axis=1, keepdims=True)
    out_ref[0:ROWS, :] = (vectors * lax.rsqrt(norms + 1e-06)).astype(jnp.bfloat16)
    labels = (target_ref[...] >> CLUSTER_SHIFT).astype(jnp.float32)
    out_ref[ROWS:, 0:ROWS] = jnp.broadcast_to(labels, (LABEL_ROWS, ROWS)).astype(jnp.bfloat16)
    out_ref[ROWS:, ROWS:] = jnp.zeros((LABEL_ROWS, WIDTH - ROWS), jnp.bfloat16)


def pack(embeddings, destination):
    return pl.pallas_call(
        pack_body,
        out_shape=pltpu.VMEM((ROWS + LABEL_ROWS, WIDTH), jnp.bfloat16),
        name="pack",
    )(embeddings, destination.reshape(1, ROWS))


def parts(start=0):
    return [slice(start + s, start + s + LANES) for s in range(0, ROWS - start, LANES)]


def pairs_body(work, mine_used, other_used, earlier, last, *refs):
    core, bits = core_index(), high_bits()
    count = len(mine_used) + len(other_used)
    mine = dict(zip(mine_used, refs))
    other = dict(zip(other_used, refs[len(mine_used) : count]))
    before_ref = refs[count] if earlier else None
    outs, (labels_ref, row_sums, column_sums, table) = refs[count + earlier : -4], refs[-4:]
    firsts = sorted({a for _, a, *_ in work})
    at = {a: n for n, a in enumerate(firsts)}
    row_sums[...] = jnp.zeros_like(row_sums)
    column_sums[...] = jnp.zeros_like(column_sums)

    def row_labels(ref):
        return ref[ROWS:, 0:ROWS].astype(jnp.float32)[0:1]

    for a in firsts:
        labels = row_labels(mine[a])
        for part in parts():
            labels_ref[at[a], part, :] = jnp.broadcast_to(labels[:, part], (LANES, LANES)).T

    def weights(a, a_rows, b_ref, b_rows, b_labels):
        scores = lax.dot_general(
            mine[a][a_rows], b_ref[b_rows], (((1,), (1,)), ((), ())), preferred_element_type=jnp.float32
        )
        left = labels_ref[at[a], a_rows, :]
        return [
            jnp.where(left == right, jnp.exp2(scores[:, n * LANES : (n + 1) * LANES] * EXP2_SCALE), 0.0)
            for n, right in enumerate(b_labels)
        ]

    def down(value):
        return jnp.sum(value.reshape(-1, 8, LANES), axis=0)

    for kind, a, is_mine, b, axis in work:
        b_ref = mine[b] if is_mine else other[b]
        slot = b if is_mine else BLOCKS + b
        labels = row_labels(b_ref)
        everything = slice(0, ROWS)
        if kind == "half":
            low, high = parts()
            (value,) = weights(a, low, b_ref, high, [labels[:, high]])
            row_sums[at[a], low, :] += value
            column_sums[slot, :, high] += down(value)
            which = core if axis is None else bits[axis]
            same = pl.ds(pl.multiple_of(which * LANES, LANES), LANES)
            chosen = jnp.where(which == 0, labels[:, low], labels[:, high])
            (value,) = weights(a, same, b_ref, same, [chosen])
            row_sums[at[a], same, :] += value
            column_sums[slot, :, same] += down(value)
            continue
        values = weights(a, everything, b_ref, everything, [labels[:, part] for part in parts()])
        if kind == "self":
            rows = lax.broadcasted_iota(jnp.int32, (ROWS, LANES), 0)
            lanes = lax.broadcasted_iota(jnp.int32, (ROWS, LANES), 1)
            values = [jnp.where(rows == lanes + n * LANES, 0.0, value) for n, value in enumerate(values)]
        else:
            for part, value in zip(parts(), values):
                column_sums[slot, :, part] += down(value)
        row_sums[at[a]] += values[0] + values[1]

    for slot in range(2 * BLOCKS):
        if last:
            rows = [table_row(c, slot) for c in (0, 1)]
            row = jnp.where(core == 0, rows[0], rows[1])
        for part in parts():
            total = jnp.sum(column_sums[slot, :, part], axis=0, keepdims=True)
            if slot in at:
                total += jnp.sum(row_sums[at[slot], part, :].T, axis=0, keepdims=True)
            if earlier:
                total += before_ref[slot, :, part]
            if last:
                table[row, :, part] = total
            else:
                outs[0][slot, :, part] = total
    if last:
        outs[0][...] = table[0 : 2 * SHARE]
        outs[1][...] = table[GIVEN : GIVEN + 2 * SHARE]
        outs[2][...] = table[HOME : HOME + 2]


def pair_sums(phase, mine, other, before):
    work = UNITS[phase]
    mine_used = sorted({a for _, a, *_ in work} | {b for _, _, is_mine, b, _ in work if is_mine})
    other_used = sorted({b for _, _, is_mine, b, _ in work if not is_mine})
    blocks = [mine[k] for k in mine_used] + [other[k] for k in other_used]
    blocks = [pltpu.with_memory_space_constraint(block, pltpu.VMEM) for block in blocks]
    before = [] if before is None else [pltpu.with_memory_space_constraint(before, pltpu.VMEM)]
    last = phase == len(PHASES) - 1
    outs = (2 * SHARE, 2 * SHARE, 2) if last else (2 * BLOCKS,)
    vmem = pl.BlockSpec(memory_space=pltpu.VMEM)
    firsts = len({a for _, a, *_ in work})
    area = sum(ROWS * ROWS // (2 if kind == "half" else 1) for kind, *_ in work)
    return pl.pallas_call(
        functools.partial(pairs_body, work, mine_used, other_used, len(before), last),
        out_shape=[pltpu.VMEM((n, 1, ROWS), jnp.float32) for n in outs],
        in_specs=[vmem] * (len(blocks) + len(before)),
        out_specs=[vmem] * len(outs),
        scratch_shapes=[
            pltpu.VMEM((firsts, ROWS, LANES), jnp.float32),
            pltpu.VMEM((firsts, ROWS, LANES), jnp.float32),
            pltpu.VMEM((2 * BLOCKS, 8, ROWS), jnp.float32),
            pltpu.VMEM((HOME + 2, 1, ROWS), jnp.float32),
        ],
        compiler_params=pltpu.CompilerParams(vmem_limit_bytes=24 * 1024 * 1024),
        cost_estimate=pl.CostEstimate(flops=2 * area * WIDTH, bytes_accessed=0, transcendentals=area),
        name=f"pair_sums_{phase}",
    )(*blocks, *before)


def core_index():
    return lax.axis_index("member") & 1


def high_bits():
    member, core = lax.axis_index("member"), core_index()
    x, y, z = member >> 2 & 1, member >> 4 & 1, lax.axis_index("cluster") >> 1
    return x, jnp.where(core == 0, y, z), jnp.where(core == 0, z, y)


def shards(embeddings, destination):
    core = core_index()
    mine = [pack(embeddings, destination)]
    mine += [None] * len(PLAN)

    def bring(k, block):
        jump = PLAN[k - 1][1]
        mine[k] = lax.ppermute(block, BOTH, fetch((jump, mirror(jump))))

    after = [k for k in range(1, BLOCKS) if PLAN[k - 1][0] == HELD_BACK]
    for k in range(1, BLOCKS):
        if k not in after:
            bring(k, mine[PLAN[k - 1][0]])
    other = {k: lax.ppermute(mine[k], BOTH, CORE_SWAP) for k in EARLY}
    (sums,) = pair_sums(0, mine, other, None)
    held, sums = lax.optimization_barrier((mine[HELD_BACK], sums))
    for k in after:
        bring(k, held)
    (sums,) = pair_sums(1, mine, other, sums)
    later, sums = lax.optimization_barrier(([mine[k] for k in LATE], sums))
    other.update({k: lax.ppermute(block, BOTH, CORE_SWAP) for k, block in zip(LATE, later)})
    (sums,) = pair_sums(2, mine, other, sums)
    kept, given, home = pair_sums(3, mine, other, sums)

    kept += lax.ppermute(given, BOTH, CORE_SWAP)
    for n in range(SHARE):
        jumps = [SHARES[c][n] for c in (0, 1)]
        home += lax.ppermute(kept[2 * n : 2 * n + 2], BOTH, give(jumps))
    density = home + lax.ppermute(home, BOTH, CORE_SWAP)
    return jnp.log1p(jnp.where(core == 0, density[0, 0], density[1, 0]))


def solution(mesh):
    in_specs = (P(BOTH, None), P(BOTH, None))
    return jax.shard_map(shards, mesh=mesh, in_specs=in_specs, out_specs=P(BOTH), check_vma=False)
```
